128 devices in a mesh: wide: 8 (over x, core), sub: 16 (over z, y).
Axes of the slice: x: 4, y: 4, z: 4, core: 2. Of those that a mesh axis runs over, the one named last changes fastest.
Arguments:
- weights: bfloat16 [16384, 128, 128], P(('wide', 'sub')), may hold values from -6 to 6
- tables: bfloat16 [8, 16, 128, 128], replicated, may hold values from -0.375 to 0.375
- pattern_first: int32 [4, 16384, 2], P(None, ('wide', 'sub')), may hold values from 0 to 15
- pattern_second: int32 [4, 16384, 2], P(None, ('wide', 'sub')), may hold values from 0 to 15
Outputs:
- result: bfloat16 [16384, 128, 128], P(('wide', 'sub'))
The draws below stay inside these ranges and needn't reach their ends.
All inputs are finite; a program needn't handle non-finite values.
Results may differ from the reference program's by a relative error of at most 0.0086.
Values may be sent and summed in bfloat16 or wider, within the bound.
No kernel may reach another device: no remote copies, remote signals or barrier semaphores. Data moves between devices by JAX's collectives and lax.ppermute only.
A program may use at most 128 MiB of HBM per device.

```python
import jax
import jax.numpy as jnp
from jax import lax

RANK = 64
NTAB = 16
LEVELS = 4
BOX_DEV = 128
COLS = 128
BOXES = 16384
DEVICES = 128


def plant(entries, own_key, least, high):
    place = [jax.random.randint(jax.random.fold_in(own_key, axis), (), 0, length) for axis, length in enumerate(entries.shape)]
    main_axis = entries.shape.index(max(entries.shape))
    beside = place[:main_axis] + [(place[main_axis] + 1) % entries.shape[main_axis]] + place[main_axis + 1:]
    return entries.at[tuple(place)].set(least).at[tuple(beside)].set(high)


def block_scale(key, shape, split, smallest, largest):
    gain = 1.0
    for dim, parts in split:
        draws = jax.random.uniform(jax.random.fold_in(jax.random.fold_in(key, 6), dim), (parts,), jnp.float32, smallest / len(split), largest / len(split))
        gain = gain * jnp.repeat(jnp.exp(draws), shape[dim] // parts).reshape((-1,) + (1,) * (len(shape) - 1 - dim))
    return gain


def noise(rng, shape, scale, limit, cuts=(), held_as=jnp.bfloat16):
    array = jax.random.normal(rng, shape, jnp.float32) * scale
    if len(cuts) > 0:
        array = block_scale(rng, shape, cuts, -0.22, 0.18) * array
    return jnp.clip(array, min=-limit, max=limit).astype(held_as)


def setup_inputs(seed: int = 0) -> dict:
    streams_of = jax.random.split(jax.random.key(seed), 5)
    weights = noise(streams_of[0], (BOXES, COLS, 2 * RANK), 1.0, 6.0, ((0, 128),))
    tables = noise(streams_of[1], (2 * LEVELS, NTAB, 2 * RANK, 2 * RANK), (4 * RANK) ** -0.5, 0.375)
    pattern_first = plant(jax.random.randint(streams_of[2], (LEVELS, BOXES, 2), 0, NTAB), jax.random.fold_in(streams_of[2], 1), 0, NTAB - 1).astype(jnp.int32)
    pattern_second = plant(jax.random.randint(streams_of[3], (LEVELS, BOXES, 2), 0, NTAB), jax.random.fold_in(streams_of[3], 1), 0, NTAB - 1).astype(jnp.int32)
    return dict(weights=weights, tables=tables, pattern_first=pattern_first, pattern_second=pattern_second)


def apply_level(field_rows, level_table, chosen, flip):
    count = field_rows.shape[0]
    shaped = field_rows.reshape((count // (2 * flip), 2, flip) + field_rows.shape[1:])
    partner = jnp.flip(shaped, 1).reshape(field_rows.shape)
    groups = count // BOX_DEV

    def per_group(items):
        local_rows, far_rows, picks = items
        block_own = jnp.take(level_table, picks[:, 0], axis=0).astype(jnp.float32)
        block_far = jnp.take(level_table, picks[:, 1], axis=0).astype(jnp.float32)
        summed = jnp.einsum("bcr,brs->bcs", local_rows.astype(jnp.float32), block_own)
        summed = summed + jnp.einsum("bcr,brs->bcs", far_rows.astype(jnp.float32), block_far)
        return summed.astype(jnp.bfloat16)

    shape_group = (groups, BOX_DEV) + field_rows.shape[1:]
    result_rows = lax.map(per_group, (field_rows.reshape(shape_group), partner.reshape(shape_group), chosen.reshape(groups, BOX_DEV, 2)))
    return result_rows.reshape(field_rows.shape)


def reference(weights, tables, pattern_first, pattern_second):
    current = weights
    for level_idx in range(LEVELS):
        current = apply_level(current, tables[level_idx], pattern_first[level_idx], BOX_DEV * 2 ** level_idx)
    spread = BOX_DEV // DEVICES
    current = current.reshape(DEVICES, DEVICES, spread, COLS, 2 * RANK).transpose(1, 0, 2, 3, 4).reshape(weights.shape)
    for level_idx in range(LEVELS):
        current = apply_level(current, tables[LEVELS + level_idx], pattern_second[level_idx], BOX_DEV // 2 ** (level_idx + 1))
    return current
```

```python
import jax
import jax.numpy as jnp
from jax import lax
from jax.experimental import pallas as pl
from jax.experimental.pallas import tpu as pltpu
from jax.sharding import PartitionSpec as P

AXES = ("wide", "sub")


def butterfly(first, second, tables, data, out, *, flips):
    boxes = data.shape[0]
    levels = len(flips) // 2

    def pick(level, term, box):
        if level < levels:
            return first[box, 2 * level + term]
        return second[2 * (level - levels) + term, box]

    for level, flip in enumerate(flips):
        source = data if level == 0 else out

        def pair(index, _, level=level, flip=flip, source=source):
            low = (index // flip) * (2 * flip) + index % flip
            high = low + flip
            rows = jnp.concatenate([source[low], source[high]], axis=1)
            own = [tables[level, pick(level, 0, low)], tables[level, pick(level, 0, high)]]
            far = [tables[level, pick(level, 1, low)], tables[level, pick(level, 1, high)]]
            blocks = jnp.concatenate(
                [jnp.concatenate([own[0], far[1]], axis=1), jnp.concatenate([far[0], own[1]], axis=1)], axis=0
            )
            summed = jnp.dot(rows, blocks, preferred_element_type=jnp.float32).astype(jnp.bfloat16)
            cols = summed.shape[1] // 2
            out[low] = summed[:, :cols]
            out[high] = summed[:, cols:]
            return 0

        lax.fori_loop(0, boxes // 2, pair, 0, unroll=4)


def local(weights, tables, pattern_first, pattern_second):
    levels = pattern_first.shape[0]
    boxes = weights.shape[0]
    first = pattern_first.transpose(1, 0, 2).reshape(boxes, 2 * levels)
    first = lax.all_to_all(first, AXES, split_axis=0, concat_axis=0, tiled=True)
    current = lax.all_to_all(weights, AXES, split_axis=0, concat_axis=0, tiled=True)
    second = pattern_second.transpose(0, 2, 1).reshape(2 * levels, boxes)
    flips = [2**level for level in range(levels)] + [boxes // 2 ** (level + 1) for level in range(levels)]
    smem = pl.BlockSpec(memory_space=pltpu.SMEM)
    vmem = pl.BlockSpec(memory_space=pltpu.VMEM)
    return pl.pallas_call(
        lambda *refs: butterfly(*refs, flips=flips),
        out_shape=jax.ShapeDtypeStruct(current.shape, current.dtype),
        in_specs=[smem, smem, vmem, vmem],
        out_specs=vmem,
        compiler_params=pltpu.CompilerParams(vmem_limit_bytes=40 * 2**20),
        cost_estimate=pl.CostEstimate(
            flops=2 * levels * boxes * 2 * 2 * 128**3, bytes_accessed=12 * 2**20, transcendentals=0
        ),
    )(first, second, tables, current)


def solution(mesh):
    in_specs = (
        P(AXES, None, None),
        P(),
        P(None, AXES, None),
        P(None, AXES, None),
    )
    out_specs = P(AXES, None, None)
    return jax.shard_map(local, mesh=mesh, in_specs=in_specs, out_specs=out_specs, check_vma=False)
```

```python
import jax
import jax.numpy as jnp
from jax import lax
from jax.experimental import pallas as pl
from jax.experimental.pallas import tpu as pltpu
from jax.sharding import PartitionSpec as P

AXES = ("wide", "sub")


def butterfly(first, second, tables, data, out, blocks, here, there, table_done, data_done, out_done, *, levels):
    boxes, cols = data.shape[0], data.shape[2]
    span = 2**levels
    apart = boxes // span
    half = boxes // 2

    def table_copy(level):
        return pltpu.make_async_copy(tables.at[level], blocks.at[level], table_done.at[level])

    def data_copy(part):
        where = pl.ds(part * half, half)
        return pltpu.make_async_copy(data.at[where], here.at[where], data_done.at[part])

    def out_copy(part, row):
        where = pl.ds(row * apart + part * (apart // 2), apart // 2)
        return pltpu.make_async_copy(here.at[where], out.at[where], out_done.at[part])

    table_copy(0).start()
    for part in range(2):
        data_copy(part).start()
    for level in range(1, 2 * levels):
        table_copy(level).start()

    def combine(level, pairs, source, target, pick):
        done = []
        for low, high in pairs:
            rows = jnp.concatenate([source[low], source[high]], axis=1)
            own = [blocks[level, pick(0, box)] for box in (low, high)]
            far = [blocks[level, pick(1, box)] for box in (low, high)]
            square = jnp.concatenate(
                [jnp.concatenate([own[0], far[1]], axis=1), jnp.concatenate([far[0], own[1]], axis=1)], axis=0
            )
            done.append(jnp.dot(rows, square, preferred_element_type=jnp.float32).astype(jnp.bfloat16))
        for (low, high), summed in zip(pairs, done):
            target[low] = summed[:, :cols]
            target[high] = summed[:, cols:]

    def split(index, flip):
        return (index // flip) * (2 * flip) + index % flip

    def before(part, _):
        data_copy(part).wait()
        for level in range(levels):
            @pl.when(part == 0)
            def _():
                table_copy(level).wait()

            source, target = (there, here) if level % 2 else (here, there)
            flip = 2**level
            lows = [part * half + split(pair, flip) for pair in range(half // 2)]
            combine(
                level,
                [(low, low + flip) for low in lows],
                source,
                target,
                lambda term, box: first[box, 2 * level + term],
            )
        return 0

    def after(part, _):
        for step in range(levels):
            level = levels + step

            @pl.when(part == 0)
            def _():
                table_copy(level).wait()

            source, target = (there, here) if level % 2 else (here, there)
            flip = span // 2 ** (step + 1)
            lows = [
                split(pair // (apart // 2), flip) * apart + part * (apart // 2) + pair % (apart // 2)
                for pair in range(half // 2)
            ]
            combine(
                level,
                [(low, low + flip * apart) for low in lows],
                source,
                target,
                lambda term, box: second[2 * step + term, box],
            )
        for row in range(span):
            out_copy(part, row).start()
        return 0

    lax.fori_loop(0, 2, before, 0)
    lax.fori_loop(0, 2, after, 0)
    for part in range(2):
        for row in range(span):
            out_copy(part, row).wait()


def local(weights, tables, pattern_first, pattern_second):
    levels, boxes = pattern_first.shape[0], weights.shape[0]
    current = lax.all_to_all(weights, AXES, split_axis=0, concat_axis=0, tiled=True)
    first = lax.all_gather(pattern_first.transpose(0, 2, 1).reshape(2 * levels, boxes), AXES)
    first = lax.dynamic_slice_in_dim(first, lax.axis_index(AXES), 1, axis=2)[:, :, 0]
    second = pattern_second.transpose(0, 2, 1).reshape(2 * levels, boxes)
    smem = pl.BlockSpec(memory_space=pltpu.SMEM)
    hbm = pl.BlockSpec(memory_space=pltpu.HBM)
    return pl.pallas_call(
        lambda *refs: butterfly(*refs, levels=levels),
        out_shape=jax.ShapeDtypeStruct(current.shape, current.dtype),
        in_specs=[smem, smem, hbm, hbm],
        out_specs=hbm,
        scratch_shapes=[
            pltpu.VMEM(tables.shape, tables.dtype),
            pltpu.VMEM(current.shape, current.dtype),
            pltpu.VMEM(current.shape, current.dtype),
            pltpu.SemaphoreType.DMA((2 * levels,)),
            pltpu.SemaphoreType.DMA((2,)),
            pltpu.SemaphoreType.DMA((2,)),
        ],
        compiler_params=pltpu.CompilerParams(vmem_limit_bytes=40 * 2**20),
        cost_estimate=pl.CostEstimate(
            flops=2 * levels * boxes * 2 * 2 * 128**3, bytes_accessed=12 * 2**20, transcendentals=0
        ),
    )(first, second, tables, current)


def solution(mesh):
    in_specs = (
        P(AXES, None, None),
        P(),
        P(None, AXES, None),
        P(None, AXES, None),
    )
    out_specs = P(AXES, None, None)
    return jax.shard_map(local, mesh=mesh, in_specs=in_specs, out_specs=out_specs, check_vma=False)
```

```python
import jax
import jax.numpy as jnp
from jax import lax
from jax.experimental import pallas as pl
from jax.experimental.pallas import tpu as pltpu
from jax.sharding import PartitionSpec as P

AXES = ("wide", "sub")
EXTRA = 8


def butterfly(first, second, tables, data, out, here, there, out_done, *, levels):
    boxes, count, cols = out.shape
    span = 2**levels
    apart = boxes // span
    half = boxes // 2

    def out_copy(part, row):
        where = pl.ds(row * apart + part * (apart // 2), apart // 2)
        return pltpu.make_async_copy(here.at[where], out.at[where], out_done.at[part])

    def combine(level, pairs, pick):
        source, target = (there, here) if level % 2 else (here if level else data, there)
        done = []
        for low, high in pairs:
            rows = jnp.concatenate([source[low, :count], source[high, :count]], axis=1)
            own = [tables[level, pick(0, box)] for box in (low, high)]
            far = [tables[level, pick(1, box)] for box in (low, high)]
            square = jnp.concatenate(
                [jnp.concatenate([own[0], far[1]], axis=1), jnp.concatenate([far[0], own[1]], axis=1)], axis=0
            )
            done.append(jnp.dot(rows, square, preferred_element_type=jnp.float32).astype(jnp.bfloat16))
        for (low, high), summed in zip(pairs, done):
            target[low] = summed[:, :cols]
            target[high] = summed[:, cols:]

    def split(index, flip):
        return (index // flip) * (2 * flip) + index % flip

    def before(part, _):
        for level in range(levels):
            flip = 2**level
            lows = [part * half + split(pair, flip) for pair in range(half // 2)]
            combine(level, [(low, low + flip) for low in lows], lambda term, box: first[box, 2 * level + term])
        return 0

    def after(part, _):
        for step in range(levels):
            flip = span // 2 ** (step + 1)
            lows = [
                split(pair // (apart // 2), flip) * apart + part * (apart // 2) + pair % (apart // 2)
                for pair in range(half // 2)
            ]
            combine(
                levels + step,
                [(low, low + flip * apart) for low in lows],
                lambda term, box: second[2 * step + term, box],
            )
        for row in range(span):
            out_copy(part, row).start()
        return 0

    lax.fori_loop(0, 2, before, 0)
    lax.fori_loop(0, 2, after, 0)
    for part in range(2):
        for row in range(span):
            out_copy(part, row).wait()


def local(weights, tables, pattern_first, pattern_second):
    levels = pattern_first.shape[0]
    boxes, count, cols = weights.shape
    picks = pattern_first.transpose(1, 0, 2).reshape(boxes, 1, 2 * levels).astype(jnp.bfloat16)
    picks = jnp.pad(picks, ((0, 0), (0, EXTRA - 1), (0, cols - 2 * levels)))
    current = jnp.concatenate([weights, picks], axis=1)
    current = lax.all_to_all(current, AXES, split_axis=0, concat_axis=0, tiled=True)
    first = current[:, count, : 2 * levels].astype(jnp.int32)
    second = pattern_second.transpose(0, 2, 1).reshape(2 * levels, boxes)
    smem = pl.BlockSpec(memory_space=pltpu.SMEM)
    vmem = pl.BlockSpec(memory_space=pltpu.VMEM)
    return pl.pallas_call(
        lambda *refs: butterfly(*refs, levels=levels),
        out_shape=jax.ShapeDtypeStruct(weights.shape, weights.dtype),
        in_specs=[smem, smem, vmem, vmem],
        out_specs=pl.BlockSpec(memory_space=pl.ANY),
        scratch_shapes=[
            pltpu.VMEM(weights.shape, weights.dtype),
            pltpu.VMEM(weights.shape, weights.dtype),
            pltpu.SemaphoreType.DMA((2,)),
        ],
        compiler_params=pltpu.CompilerParams(vmem_limit_bytes=40 * 2**20),
        cost_estimate=pl.CostEstimate(
            flops=2 * levels * boxes * 2 * 2 * 128**3, bytes_accessed=12 * 2**20, transcendentals=0
        ),
    )(first, second, tables, current)


def solution(mesh):
    in_specs = (
        P(AXES, None, None),
        P(),
        P(None, AXES, None),
        P(None, AXES, None),
    )
    out_specs = P(AXES, None, None)
    return jax.shard_map(local, mesh=mesh, in_specs=in_specs, out_specs=out_specs, check_vma=False)
```

```python
import jax
import jax.numpy as jnp
from jax import lax
from jax.experimental import pallas as pl
from jax.experimental.pallas import tpu as pltpu
from jax.sharding import PartitionSpec as P

AXES = ("wide", "sub")
EXTRA = 8
PARTS = 8


def pack(place, picks, weights, packed, held, held_done, done):
    boxes, count, cols = weights.shape
    copies = []
    for part in range(PARTS):
        where = pl.ds(part * (boxes // PARTS), boxes // PARTS)
        copies.append(pltpu.make_async_copy(weights.at[where], packed.at[where, pl.ds(0, count)], done.at[part]))
    first = pltpu.make_async_copy(picks, held, held_done)
    first.start()
    for copy in copies:
        copy.start()
    first.wait()
    shape = (boxes * EXTRA, boxes)
    chosen = lax.broadcasted_iota(jnp.int32, shape, 1) == lax.broadcasted_iota(jnp.int32, shape, 0) // EXTRA
    rows = jnp.where(chosen, jnp.tile(held[...].astype(jnp.float32), (boxes, 1)), 0.0).astype(jnp.bfloat16)
    column = (lax.broadcasted_iota(jnp.int32, (boxes, cols), 1) == place[0]).astype(jnp.bfloat16)
    spread = jnp.dot(rows, column, preferred_element_type=jnp.float32)
    packed[:, count:] = spread.astype(jnp.bfloat16).reshape(boxes, EXTRA, cols)
    for copy in copies:
        copy.wait()


def butterfly(second, tables, data, out, here, there, picks, first, first_done, out_done, *, levels):
    boxes, count, cols = out.shape
    span = 2**levels
    apart = boxes // span
    half = boxes // 2

    picks[...] = jnp.sum(data[:, count:].astype(jnp.float32), axis=0).astype(jnp.int32)
    copy = pltpu.make_async_copy(picks, first, first_done)
    copy.start()
    copy.wait()

    def out_copy(part, row):
        where = pl.ds(row * apart + part * (apart // 2), apart // 2)
        return pltpu.make_async_copy(here.at[where], out.at[where], out_done.at[part])

    def combine(level, pairs, pick):
        source, target = (there, here) if level % 2 else (here if level else data, there)
        done = []
        for low, high in pairs:
            rows = jnp.concatenate([source[low, :count], source[high, :count]], axis=1)
            own = [tables[level, pick(0, box)] for box in (low, high)]
            far = [tables[level, pick(1, box)] for box in (low, high)]
            square = jnp.concatenate(
                [jnp.concatenate([own[0], far[1]], axis=1), jnp.concatenate([far[0], own[1]], axis=1)], axis=0
            )
            done.append(jnp.dot(rows, square, preferred_element_type=jnp.float32).astype(jnp.bfloat16))
        for (low, high), summed in zip(pairs, done):
            target[low] = summed[:, :cols]
            target[high] = summed[:, cols:]

    def split(index, flip):
        return (index // flip) * (2 * flip) + index % flip

    def before(part, _):
        for level in range(levels):
            flip = 2**level
            lows = [part * half + split(pair, flip) for pair in range(half // 2)]
            combine(level, [(low, low + flip) for low in lows], lambda term, box: first[2 * level + term, box])
        return 0

    def after(part, _):
        for step in range(levels):
            flip = span // 2 ** (step + 1)
            lows = [
                split(pair // (apart // 2), flip) * apart + part * (apart // 2) + pair % (apart // 2)
                for pair in range(half // 2)
            ]
            pieces = 2 if step == levels - 1 else 1
            for piece in range(pieces):
                combine(
                    levels + step,
                    [(low, low + flip * apart) for low in lows[piece * len(lows) // pieces :][: len(lows) // pieces]],
                    lambda term, box: second[2 * step + term, box],
                )
                if step == levels - 1:
                    for row in range(piece * span // pieces, (piece + 1) * span // pieces):
                        out_copy(part, row).start()
        return 0

    lax.fori_loop(0, 2, before, 0)
    lax.fori_loop(0, 2, after, 0)
    for part in range(2):
        for row in range(span):
            out_copy(part, row).wait()


def local(weights, tables, pattern_first, pattern_second):
    levels = pattern_first.shape[0]
    boxes, count, cols = weights.shape
    place = lax.axis_index(AXES).astype(jnp.int32).reshape(1)
    first, second = (
        pattern.transpose(0, 2, 1).reshape(2 * levels, boxes) for pattern in (pattern_first, pattern_second)
    )
    smem = pl.BlockSpec(memory_space=pltpu.SMEM)
    vmem = pl.BlockSpec(memory_space=pltpu.VMEM)
    whole = pl.BlockSpec(memory_space=pl.ANY)
    current = pl.pallas_call(
        pack,
        out_shape=jax.ShapeDtypeStruct((boxes, count + EXTRA, cols), weights.dtype),
        in_specs=[smem, whole, whole],
        out_specs=vmem,
        scratch_shapes=[
            pltpu.VMEM(first.shape, first.dtype),
            pltpu.SemaphoreType.DMA,
            pltpu.SemaphoreType.DMA((PARTS,)),
        ],
        compiler_params=pltpu.CompilerParams(vmem_limit_bytes=16 * 2**20),
    )(place, *(pltpu.with_memory_space_constraint(array, pltpu.HBM) for array in (first, weights)))
    current = lax.all_to_all(current, AXES, split_axis=0, concat_axis=0, tiled=True)
    return pl.pallas_call(
        lambda *refs: butterfly(*refs, levels=levels),
        out_shape=jax.ShapeDtypeStruct(weights.shape, weights.dtype),
        in_specs=[smem, vmem, vmem],
        out_specs=whole,
        scratch_shapes=[
            pltpu.VMEM(weights.shape, weights.dtype),
            pltpu.VMEM(weights.shape, weights.dtype),
            pltpu.VMEM(first.shape, first.dtype),
            pltpu.SMEM(first.shape, first.dtype),
            pltpu.SemaphoreType.DMA,
            pltpu.SemaphoreType.DMA((2,)),
        ],
        compiler_params=pltpu.CompilerParams(vmem_limit_bytes=40 * 2**20),
        cost_estimate=pl.CostEstimate(
            flops=2 * levels * boxes * 2 * 2 * 128**3, bytes_accessed=12 * 2**20, transcendentals=0
        ),
    )(second, tables, current)


def solution(mesh):
    in_specs = (
        P(AXES, None, None),
        P(),
        P(None, AXES, None),
        P(None, AXES, None),
    )
    out_specs = P(AXES, None, None)
    return jax.shard_map(local, mesh=mesh, in_specs=in_specs, out_specs=out_specs, check_vma=False)
```

```python
import jax
import jax.numpy as jnp
from jax import lax
from jax.experimental import pallas as pl
from jax.experimental.pallas import tpu as pltpu
from jax.sharding import PartitionSpec as P

AXES = ("wide", "sub")
EXTRA = 8
PARTS = 8


def pack(place, picks, weights, packed, held, held_done, done):
    boxes, count, cols = weights.shape
    copies = []
    for part in range(PARTS):
        where = pl.ds(part * (boxes // PARTS), boxes // PARTS)
        copies.append(pltpu.make_async_copy(weights.at[where], packed.at[where, pl.ds(0, count)], done.at[part]))
    first = pltpu.make_async_copy(picks, held, held_done)
    first.start()
    for copy in copies:
        copy.start()
    first.wait()
    shape = (boxes * EXTRA, boxes)
    chosen = lax.broadcasted_iota(jnp.int32, shape, 1) == lax.broadcasted_iota(jnp.int32, shape, 0) // EXTRA
    rows = jnp.where(chosen, jnp.tile(held[...].astype(jnp.float32), (boxes, 1)), 0.0).astype(jnp.bfloat16)
    column = (lax.broadcasted_iota(jnp.int32, (boxes, cols), 1) == place[0]).astype(jnp.bfloat16)
    spread = jnp.dot(rows, column, preferred_element_type=jnp.float32)
    packed[:, count:] = spread.astype(jnp.bfloat16).reshape(boxes, EXTRA, cols)
    for copy in copies:
        copy.wait()


def butterfly(
    picks_after, tables, data, out, here, there, picks, first, second, first_done, second_done, out_done, *, levels
):
    boxes, count, cols = out.shape
    span = 2**levels
    apart = boxes // span
    half = boxes // 2

    later = pltpu.make_async_copy(picks_after, second, second_done)
    later.start()
    picks[...] = jnp.sum(data[:, count:].astype(jnp.float32), axis=0).astype(jnp.int32)
    copy = pltpu.make_async_copy(picks, first, first_done)
    copy.start()
    copy.wait()

    def out_copy(part, row):
        where = pl.ds(row * apart + part * (apart // 2), apart // 2)
        return pltpu.make_async_copy(here.at[where], out.at[where], out_done.at[part])

    def combine(level, pairs, pick):
        source, target = (there, here) if level % 2 else (here if level else data, there)
        done = []
        for low, high in pairs:
            rows = jnp.concatenate([source[low, :count], source[high, :count]], axis=1)
            own = [tables[level, pick(0, box)] for box in (low, high)]
            far = [tables[level, pick(1, box)] for box in (low, high)]
            square = jnp.concatenate(
                [jnp.concatenate([own[0], far[1]], axis=1), jnp.concatenate([far[0], own[1]], axis=1)], axis=0
            )
            done.append(jnp.dot(rows, square, preferred_element_type=jnp.float32).astype(jnp.bfloat16))
        for (low, high), summed in zip(pairs, done):
            target[low] = summed[:, :cols]
            target[high] = summed[:, cols:]

    def split(index, flip):
        return (index // flip) * (2 * flip) + index % flip

    def before(part, _):
        for level in range(levels):
            flip = 2**level
            lows = [part * half + split(pair, flip) for pair in range(half // 2)]
            combine(level, [(low, low + flip) for low in lows], lambda term, box: first[2 * level + term, box])
        return 0

    def after(part, _):
        for step in range(levels):
            flip = span // 2 ** (step + 1)
            lows = [
                split(pair // (apart // 2), flip) * apart + part * (apart // 2) + pair % (apart // 2)
                for pair in range(half // 2)
            ]
            pieces = 4 if step == levels - 1 else 1
            for piece in range(pieces):
                combine(
                    levels + step,
                    [(low, low + flip * apart) for low in lows[piece * len(lows) // pieces :][: len(lows) // pieces]],
                    lambda term, box: second[2 * step + term, box],
                )
                if step == levels - 1:
                    for row in range(piece * span // pieces, (piece + 1) * span // pieces):
                        out_copy(part, row).start()
        return 0

    lax.fori_loop(0, 2, before, 0)
    later.wait()
    lax.fori_loop(0, 2, after, 0)
    for part in range(2):
        for row in range(span):
            out_copy(part, row).wait()


def local(weights, tables, pattern_first, pattern_second):
    levels = pattern_first.shape[0]
    boxes, count, cols = weights.shape
    place = lax.axis_index(AXES).astype(jnp.int32).reshape(1)
    first, second = (
        pattern.transpose(0, 2, 1).reshape(2 * levels, boxes) for pattern in (pattern_first, pattern_second)
    )
    smem = pl.BlockSpec(memory_space=pltpu.SMEM)
    vmem = pl.BlockSpec(memory_space=pltpu.VMEM)
    whole = pl.BlockSpec(memory_space=pl.ANY)
    current = pl.pallas_call(
        pack,
        out_shape=jax.ShapeDtypeStruct((boxes, count + EXTRA, cols), weights.dtype),
        in_specs=[smem, whole, whole],
        out_specs=vmem,
        scratch_shapes=[
            pltpu.VMEM(first.shape, first.dtype),
            pltpu.SemaphoreType.DMA,
            pltpu.SemaphoreType.DMA((PARTS,)),
        ],
        compiler_params=pltpu.CompilerParams(vmem_limit_bytes=16 * 2**20),
    )(place, *(pltpu.with_memory_space_constraint(array, pltpu.HBM) for array in (first, weights)))
    current = lax.all_to_all(current, AXES, split_axis=0, concat_axis=0, tiled=True)
    return pl.pallas_call(
        lambda *refs: butterfly(*refs, levels=levels),
        out_shape=jax.ShapeDtypeStruct(weights.shape, weights.dtype),
        in_specs=[whole, vmem, vmem],
        out_specs=whole,
        scratch_shapes=[
            pltpu.VMEM(weights.shape, weights.dtype),
            pltpu.VMEM(weights.shape, weights.dtype),
            pltpu.VMEM(first.shape, first.dtype),
            pltpu.SMEM(first.shape, first.dtype),
            pltpu.SMEM(second.shape, second.dtype),
            pltpu.SemaphoreType.DMA,
            pltpu.SemaphoreType.DMA,
            pltpu.SemaphoreType.DMA((2,)),
        ],
        compiler_params=pltpu.CompilerParams(vmem_limit_bytes=40 * 2**20),
        cost_estimate=pl.CostEstimate(
            flops=2 * levels * boxes * 2 * 2 * 128**3, bytes_accessed=12 * 2**20, transcendentals=0
        ),
    )(second, tables, current)


def solution(mesh):
    in_specs = (
        P(AXES, None, None),
        P(),
        P(None, AXES, None),
        P(None, AXES, None),
    )
    out_specs = P(AXES, None, None)
    return jax.shard_map(local, mesh=mesh, in_specs=in_specs, out_specs=out_specs, check_vma=False)
```

```python
import jax
import jax.numpy as jnp
from jax import lax
from jax.experimental import pallas as pl
from jax.experimental.pallas import tpu as pltpu
from jax.sharding import PartitionSpec as P

AXES = ("wide", "sub")
EXTRA = 2
PARTS = 8


def pack(place, picks, weights, packed, held, held_done, done):
    boxes, pairs, _, cols = weights.shape
    groups = held.shape[0] // EXTRA
    copies = []
    for part in range(PARTS):
        where = pl.ds(part * (boxes // PARTS), boxes // PARTS)
        copies.append(pltpu.make_async_copy(weights.at[where], packed.at[where, pl.ds(0, pairs)], done.at[part]))
    first = pltpu.make_async_copy(picks, held, held_done)
    first.start()
    for copy in copies:
        copy.start()
    first.wait()
    row = lax.broadcasted_iota(jnp.int32, (boxes * EXTRA, boxes), 0)
    chosen = lax.broadcasted_iota(jnp.int32, row.shape, 1) == (row >> 1)
    column = lax.broadcasted_iota(jnp.int32, (boxes, cols), 1)
    width = cols // groups
    values = held[...].astype(jnp.float32)
    spread = jnp.zeros((boxes * EXTRA, cols), jnp.float32)
    for group in range(groups):
        even, odd = values[2 * group : 2 * group + 1], values[2 * group + 1 : 2 * group + 2]
        rows = jnp.where(chosen, jnp.where((row & 1) == 0, even, odd), 0.0).astype(jnp.bfloat16)
        target = (column == group * width + (place[0] & (width - 1))).astype(jnp.bfloat16)
        spread = spread + jnp.dot(rows, target, preferred_element_type=jnp.float32)
    packed[:, pairs] = spread.astype(jnp.bfloat16).reshape(boxes, EXTRA, cols)
    for copy in copies:
        copy.wait()


def butterfly(
    picks_after, tables, data, message, out, here, there, picks, first, second, first_done, second_done, out_done, *, levels
):
    boxes, count, cols = out.shape
    span = 2**levels
    apart = boxes // span
    half = boxes // 2

    later = pltpu.make_async_copy(picks_after, second, second_done)
    later.start()
    groups = picks.shape[0] // EXTRA
    width = boxes // groups
    sums = [
        jnp.sum(message[group * width : (group + 1) * width, count // 2].astype(jnp.float32), axis=0)
        for group in range(groups)
    ]
    picks[...] = jnp.concatenate(sums, axis=0).astype(jnp.int32)
    copy = pltpu.make_async_copy(picks, first, first_done)
    copy.start()
    copy.wait()

    def out_copy(part, row):
        where = pl.ds(row * apart + part * (apart // 2), apart // 2)
        return pltpu.make_async_copy(here.at[where], out.at[where], out_done.at[part])

    def combine(level, pairs, pick, read=None):
        source, target = (there, here) if level % 2 else (here, there)
        done = []
        for index, (low, high) in enumerate(pairs):
            rows = jnp.concatenate(read(index) if read else [source[low], source[high]], axis=1)
            own = [tables[level, pick(0, box)] for box in (low, high)]
            far = [tables[level, pick(1, box)] for box in (low, high)]
            square = jnp.concatenate(
                [jnp.concatenate([own[0], far[1]], axis=1), jnp.concatenate([far[0], own[1]], axis=1)], axis=0
            )
            done.append(jnp.dot(rows, square, preferred_element_type=jnp.float32).astype(jnp.bfloat16))
        for (low, high), summed in zip(pairs, done):
            target[low] = summed[:, :cols]
            target[high] = summed[:, cols:]

    def split(index, flip):
        return (index // flip) * (2 * flip) + index % flip

    def before(part, _):
        for level in range(levels):
            flip = 2**level
            lows = [part * half + split(pair, flip) for pair in range(half // 2)]
            arrived = data.at[pl.ds(pl.multiple_of(part * half * (count + EXTRA), 128), half * (count + EXTRA))]
            combine(
                level,
                [(low, low + flip) for low in lows],
                lambda term, box: first[2 * (box // width) + term, level * width + box % width],
                None
                if level
                else lambda index: [
                    arrived[pl.ds((split(index, flip) + side) * (count + EXTRA), count), :]
                    for side in (0, flip)
                ],
            )
        return 0

    def after(part, _):
        for step in range(levels):
            flip = span // 2 ** (step + 1)
            lows = [
                split(pair // (apart // 2), flip) * apart + part * (apart // 2) + pair % (apart // 2)
                for pair in range(half // 2)
            ]
            pieces = 4 if step == levels - 1 else 1
            for piece in range(pieces):
                combine(
                    levels + step,
                    [(low, low + flip * apart) for low in lows[piece * len(lows) // pieces :][: len(lows) // pieces]],
                    lambda term, box: second[2 * step + term, box],
                )
                if step == levels - 1:
                    for row in range(piece * span // pieces, (piece + 1) * span // pieces):
                        out_copy(part, row).start()
        return 0

    lax.fori_loop(0, 2, before, 0)
    later.wait()
    lax.fori_loop(0, 2, after, 0)
    for part in range(2):
        for row in range(span):
            out_copy(part, row).wait()


def local(weights, tables, pattern_first, pattern_second):
    levels = pattern_first.shape[0]
    boxes, count, cols = weights.shape
    place = lax.axis_index(AXES).astype(jnp.int32).reshape(1)
    first, second = (
        pattern.transpose(0, 2, 1).reshape(2 * levels, boxes) for pattern in (pattern_first, pattern_second)
    )
    smem = pl.BlockSpec(memory_space=pltpu.SMEM)
    vmem = pl.BlockSpec(memory_space=pltpu.VMEM)
    whole = pl.BlockSpec(memory_space=pl.ANY)
    current = pl.pallas_call(
        pack,
        out_shape=jax.ShapeDtypeStruct((boxes, (count + EXTRA) // 2, 2, cols), weights.dtype),
        in_specs=[smem, whole, whole],
        out_specs=vmem,
        scratch_shapes=[
            pltpu.VMEM(first.shape, first.dtype),
            pltpu.SemaphoreType.DMA,
            pltpu.SemaphoreType.DMA((PARTS,)),
        ],
        compiler_params=pltpu.CompilerParams(vmem_limit_bytes=16 * 2**20),
    )(place, *(pltpu.with_memory_space_constraint(array, pltpu.HBM) for array in (first, weights.reshape(boxes, count // 2, 2, cols))))
    current = lax.all_to_all(current, AXES, split_axis=0, concat_axis=0, tiled=True)
    return pl.pallas_call(
        lambda *refs: butterfly(*refs, levels=levels),
        out_shape=jax.ShapeDtypeStruct(weights.shape, weights.dtype),
        in_specs=[whole, vmem, vmem, vmem],
        out_specs=whole,
        scratch_shapes=[
            pltpu.VMEM(weights.shape, weights.dtype),
            pltpu.VMEM(weights.shape, weights.dtype),
            pltpu.VMEM(first.shape, first.dtype),
            pltpu.SMEM(first.shape, first.dtype),
            pltpu.SMEM(second.shape, second.dtype),
            pltpu.SemaphoreType.DMA,
            pltpu.SemaphoreType.DMA,
            pltpu.SemaphoreType.DMA((2,)),
        ],
        compiler_params=pltpu.CompilerParams(vmem_limit_bytes=40 * 2**20),
        cost_estimate=pl.CostEstimate(
            flops=2 * levels * boxes * 2 * 2 * 128**3, bytes_accessed=12 * 2**20, transcendentals=0
        ),
    )(second, tables, current.reshape(boxes * (count + EXTRA), cols), current)


def solution(mesh):
    in_specs = (
        P(AXES, None, None),
        P(),
        P(None, AXES, None),
        P(None, AXES, None),
    )
    out_specs = P(AXES, None, None)
    return jax.shard_map(local, mesh=mesh, in_specs=in_specs, out_specs=out_specs, check_vma=False)
```
